1024 devices in a mesh: dp: 32 (over y, z_hi), mp: 32 (over z_lo, x, core).
Axes of the slice: x: 8, y: 8, z: 8 (z_hi: 4, z_lo: 2; z = z_hi * 2 + z_lo), core: 2. Of those that a mesh axis runs over, the one named last changes fastest.
Arguments:
- image_emb: bfloat16 [196608, 1152], P(('dp', 'mp')), may hold values from -0.1875 to 0.1875
- text_emb: bfloat16 [196608, 1152], P(('dp', 'mp')), may hold values from -0.1875 to 0.1875
- log_scale: float32 [1], replicated, may hold values from 1.6 to 3
- bias: float32 [1], replicated, may hold values from -4 to -1
Outputs:
- image_grad: float32 [196608, 1152], P(('dp', 'mp'))
- text_grad: float32 [196608, 1152], P(('dp', 'mp'))
The draws below stay inside these ranges and needn't reach their ends.
All inputs are finite; a program needn't handle non-finite values.
Results may differ from the reference program's by a relative error of at most 0.0033.
Values may be sent and summed in bfloat16 or wider, within the bound.
No kernel may reach another device: no remote copies, remote signals or barrier semaphores. Data moves between devices by JAX's collectives and lax.ppermute only.
A program may use at most 32 MiB of HBM per device.

```python
import jax
import jax.numpy as jnp

D = 1152
ROWS = 192
SHIFTS = 4
BLOCKS = 1024
PAIRS = 196608


def level_of(own_key, dims, split, low, high):
    def one(position, shards_of):
        steps = jax.random.uniform(jax.random.fold_in(jax.random.fold_in(own_key, 6), position), (shards_of,), jnp.float32, low / len(split), high / len(split))
        return jnp.repeat(jnp.exp(steps), dims[position] // shards_of).reshape((-1,) + (1,) * (len(dims) - position - 1))

    loudness = one(*split[0])
    for cut in split[1:]:
        loudness = loudness * one(*cut)
    return loudness


def bell_draw(own_key, dims, spread, reach, shards=(), kind=jnp.bfloat16):
    drawn = jax.random.normal(own_key, dims, jnp.float32) * spread
    if len(shards) > 0:
        drawn = level_of(own_key, dims, shards, -0.22, 0.18) * drawn
    return jnp.clip(drawn, min=-reach, max=reach).astype(kind)


def setup_inputs(seed: int = 0) -> dict:
    keys = jax.random.split(jax.random.key(seed), 5)
    return {
        "image_emb": bell_draw(keys[0], (PAIRS, D), D ** -0.5, 0.1875, ((0, 1024),)),
        "text_emb": bell_draw(keys[1], (PAIRS, D), D ** -0.5, 0.1875, ((0, 1024),)),
        "log_scale": jnp.clip(jax.random.uniform(keys[2], (1,), jnp.float32, 1.6, 3.0), 1.6, 3.0),
        "bias": jnp.clip(jax.random.uniform(keys[3], (1,), jnp.float32, -4.0, -1.0), -4.0, -1.0),
    }


def reference(image_emb, text_emb, log_scale, bias):
    scale = jnp.exp(log_scale[0])
    offset = bias[0]
    images = image_emb.astype(jnp.float32).reshape(BLOCKS, ROWS, D)
    texts = text_emb.astype(jnp.float32).reshape(BLOCKS, ROWS, D)
    image_grad = jnp.zeros((BLOCKS, ROWS, D), jnp.float32)
    text_grad = jnp.zeros((BLOCKS, ROWS, D), jnp.float32)
    identity = jnp.eye(ROWS, dtype=jnp.float32)
    for step in range(SHIFTS + 1):
        moved = jnp.roll(texts, step, axis=0)
        logits = scale * jnp.einsum("nrd,ncd->nrc", images, moved) + offset
        target = identity if step == 0 else jnp.zeros_like(identity)
        weights = (scale * (jax.nn.sigmoid(logits) - target)).astype(jnp.bfloat16).astype(jnp.float32)
        image_grad = image_grad + jnp.einsum("nrc,ncd->nrd", weights, moved)
        text_grad = text_grad + jnp.roll(jnp.einsum("nrc,nrd->ncd", weights, images), -step, axis=0)
    return image_grad.reshape(PAIRS, D), text_grad.reshape(PAIRS, D)
```

```python
import jax
import jax.numpy as jnp
from jax import lax
from jax.experimental import pallas as pl
from jax.experimental.pallas import tpu as pltpu
from jax.sharding import PartitionSpec as P

AXES = ("dp", "mp")
VMEM = pl.BlockSpec(memory_space=pltpu.VMEM)
SMEM = pl.BlockSpec(memory_space=pltpu.SMEM)
ANY = pl.BlockSpec(memory_space=pl.ANY)
HBM = pl.BlockSpec(memory_space=pltpu.HBM)
NT = (((1,), (1,)), ((), ()))


def on_core_1():
    return lax.rem(lax.axis_index("mp"), 2) == 1


def weights(fixed, moving, log_scale, bias, own=False):
    inner = lax.dot_general(fixed, moving, NT, preferred_element_type=jnp.float32)
    scale = jnp.exp(jnp.full((1, inner.shape[1]), log_scale, jnp.float32))
    chance = jax.nn.sigmoid(scale * inner + bias)
    if own:
        row_ids = lax.broadcasted_iota(jnp.int32, inner.shape, 0)
        col_ids = lax.broadcasted_iota(jnp.int32, inner.shape, 1)
        chance = chance - jnp.where(row_ids == col_ids, 1.0, 0.0)
    return (scale * chance).astype(jnp.bfloat16)


def product(left, right):
    return jnp.dot(left, right, preferred_element_type=jnp.float32)


def choose_kernel(image, text, moving, fixed, sems):
    def copies(first, second):
        one = pltpu.make_async_copy(first, moving, sems.at[0])
        two = pltpu.make_async_copy(second, fixed, sems.at[1])
        one.start()
        two.start()
        one.wait()
        two.wait()

    core_1 = on_core_1()

    @pl.when(core_1)
    def _():
        copies(text, image)

    @pl.when(jnp.logical_not(core_1))
    def _():
        copies(image, text)


def own_kernel(log_scale, bias, fixed, moving, second, fixed_sum, moving_sum):
    ls, off = log_scale[0], bias[0]
    fixed_sum[...] = product(weights(fixed[...], moving[...], ls, off, True), moving[...])
    fixed_sum[...] += product(weights(fixed[...], second[...], ls, off), second[...])
    moving_sum[...] = product(weights(moving[...], fixed[...], ls, off, True), fixed[...])


def middle_kernel(log_scale, bias, fixed, other, block, fixed_in, *rest):
    ls, off = log_scale[0], bias[0]
    other_in, (fixed_sum, other_sum) = rest[:-2], rest[-2:]
    term = product(weights(other[...], block[...], ls, off), block[...])
    for ref in other_in:
        term = term + ref[...]
    other_sum[...] = term
    fixed_sum[...] = fixed_in[...] + product(weights(fixed[...], block[...], ls, off), block[...])


def other_kernel(log_scale, bias, other, block, other_in, other_sum):
    ls, off = log_scale[0], bias[0]
    term = other_in[...] + product(weights(other[...], block[...], ls, off), block[...])
    other_sum[...] = term.astype(other_sum.dtype)


def last_kernel(log_scale, bias, fixed, moving, block4, block5, fixed_in, moving_in, other_in, image_out, text_out, fixed_sum, moving_sum, sems):
    ls, off = log_scale[0], bias[0]
    fixed_sum[...] = fixed_in[...] + product(weights(fixed[...], block4[...], ls, off), block4[...])
    moving_sum[...] = moving_in[...] + other_in[...].astype(jnp.float32) + product(weights(moving[...], block5[...], ls, off), block5[...])

    def copies(fixed_out, moving_out):
        one = pltpu.make_async_copy(fixed_sum, fixed_out, sems.at[0])
        two = pltpu.make_async_copy(moving_sum, moving_out, sems.at[1])
        one.start()
        two.start()
        one.wait()
        two.wait()

    core_1 = on_core_1()

    @pl.when(core_1)
    def _():
        copies(image_out, text_out)

    @pl.when(jnp.logical_not(core_1))
    def _():
        copies(text_out, image_out)


def call(body, outs, n_in, products, **more):
    return pl.pallas_call(
        body,
        out_shape=outs,
        in_specs=[SMEM, SMEM] + [VMEM] * n_in,
        out_specs=more.pop("out_specs", [VMEM] * len(outs)),
        compiler_params=pltpu.CompilerParams(vmem_limit_bytes=24 << 20),
        cost_estimate=pl.CostEstimate(flops=products * 85_000_000, bytes_accessed=1 << 20, transcendentals=0),
        **more,
    )


def local(image_emb, text_emb, log_scale, bias):
    n = lax.axis_size("dp") * lax.axis_size("mp")
    same = [(i, (i + 2) % n if i % 2 else (i - 2) % n) for i in range(n)]
    cross = [(i, (i - 1) % n if i % 2 == 0 else (i + 1) % n) for i in range(n)]
    split = [(i, (i + 3) % n if i % 2 == 0 else (i - 3) % n) for i in range(n)]
    swap = [(i, i ^ 1) for i in range(n)]
    block = jax.ShapeDtypeStruct(image_emb.shape, jnp.bfloat16)
    total = jax.ShapeDtypeStruct(image_emb.shape, jnp.float32)

    moving, fixed = pl.pallas_call(
        choose_kernel,
        out_shape=[pltpu.VMEM(block.shape, block.dtype)] * 2,
        in_specs=[HBM, HBM],
        out_specs=[VMEM, VMEM],
        scratch_shapes=[pltpu.SemaphoreType.DMA((2,))],
    )(pltpu.with_memory_space_constraint(image_emb, pltpu.HBM), pltpu.with_memory_space_constraint(text_emb, pltpu.HBM))

    block2 = lax.ppermute(moving, AXES, same)
    second = lax.ppermute(fixed, AXES, swap)
    other = lax.ppermute(moving, AXES, swap)
    block3 = lax.ppermute(fixed, AXES, split)
    block4 = lax.ppermute(block2, AXES, same)
    block5 = lax.ppermute(block3, AXES, cross)

    fixed_sum, moving_sum = call(own_kernel, [total, total], 3, 6)(log_scale, bias, fixed, moving, second)
    fixed_sum, other_sum = call(middle_kernel, [total, total], 4, 4)(log_scale, bias, fixed, other, block2, fixed_sum)
    fixed_sum, other_sum = call(middle_kernel, [total, total], 5, 4)(log_scale, bias, fixed, other, block3, fixed_sum, other_sum)
    (sent,) = call(other_kernel, [block], 3, 2)(log_scale, bias, other, block4, other_sum)
    other_sum = lax.ppermute(sent, AXES, swap)
    image_grad, text_grad = call(
        last_kernel,
        [total, total],
        7,
        4,
        out_specs=[ANY, ANY],
        scratch_shapes=[
            pltpu.VMEM(image_emb.shape, jnp.float32),
            pltpu.VMEM(image_emb.shape, jnp.float32),
            pltpu.SemaphoreType.DMA((2,)),
        ],
    )(log_scale, bias, fixed, moving, block4, block5, fixed_sum, moving_sum, other_sum)
    return (image_grad, text_grad)


def solution(mesh):
    return jax.shard_map(
        local,
        mesh=mesh,
        in_specs=(P(("dp", "mp"), None), P(("dp", "mp"), None), P(), P()),
        out_specs=(P(("dp", "mp"), None), P(("dp", "mp"), None)),
        check_vma=False,
    )
```

```python
import jax
import jax.numpy as jnp
from jax import lax
from jax.experimental import pallas as pl
from jax.experimental.pallas import tpu as pltpu
from jax.sharding import PartitionSpec as P

AXES = ("dp", "mp")
VMEM = pl.BlockSpec(memory_space=pltpu.VMEM)
SMEM = pl.BlockSpec(memory_space=pltpu.SMEM)
HBM = pl.BlockSpec(memory_space=pltpu.HBM)
PIECES = 3
NT = (((1,), (1,)), ((), ()))


def on_core_1():
    return lax.rem(lax.axis_index("mp"), 2) == 1


def weights(fixed, moving, scalars, own=False):
    inner = lax.dot_general(fixed, moving, NT, preferred_element_type=jnp.float32)
    scale, bias = scalars[0:1, :], scalars[1:2, :]
    chance = jax.nn.sigmoid(scale * inner + bias)
    if own:
        row_ids = lax.broadcasted_iota(jnp.int32, inner.shape, 0)
        col_ids = lax.broadcasted_iota(jnp.int32, inner.shape, 1)
        chance = chance - jnp.where(row_ids == col_ids, 1.0, 0.0)
    return (scale * chance).astype(jnp.bfloat16)


def product(left, right):
    return jnp.dot(left, right, preferred_element_type=jnp.float32)


def choose_kernel(image, text, moving, fixed, sems):
    def copies(first, second):
        one = pltpu.make_async_copy(first, moving, sems.at[0])
        two = pltpu.make_async_copy(second, fixed, sems.at[1])
        one.start()
        two.start()
        one.wait()
        two.wait()

    core_1 = on_core_1()

    @pl.when(core_1)
    def _():
        copies(text, image)

    @pl.when(jnp.logical_not(core_1))
    def _():
        copies(image, text)


def own_kernel(log_scale, bias, fixed, moving, scalars, fixed_sum, moving_sum, fixed_copy, both):
    fixed_copy[...] = fixed[...]
    both[0] = fixed[...]
    both[1] = moving[...]
    scalars[0:1, :] = jnp.exp(jnp.full((1, scalars.shape[1]), log_scale[0], jnp.float32))
    scalars[1:2, :] = jnp.full((1, scalars.shape[1]), bias[0], jnp.float32)
    fixed_sum[...] = product(weights(fixed[...], moving[...], scalars, True), moving[...])
    moving_sum[...] = product(weights(moving[...], fixed[...], scalars, True), fixed[...])


def first_kernel(scalars, fixed, block, fixed_in, fixed_sum):
    fixed_sum[...] = fixed_in[...] + product(weights(fixed[...], block[...], scalars), block[...])


def second_kernel(scalars, fixed, swapped, block, fixed_in, fixed_sum, other_sum):
    second, other = swapped.at[0], swapped.at[1]
    other_sum[...] = product(weights(other[...], block[...], scalars), block[...])
    fixed_sum[...] = fixed_in[...] + product(weights(fixed[...], second[...], scalars), second[...])


def third_kernel(scalars, fixed, swapped, block, fixed_in, other_in, fixed_sum, other_sum):
    other_sum[...] = other_in[...] + product(weights(swapped[1], block[...], scalars), block[...])
    fixed_sum[...] = fixed_in[...] + product(weights(fixed[...], block[...], scalars), block[...])


def other_kernel(scalars, swapped, block, other_in, other_sum):
    term = other_in[...] + product(weights(swapped[1], block[...], scalars), block[...])
    other_sum[...] = term.astype(other_sum.dtype)


def add_and_write(weight, block, earlier, total, out, sems):
    wide = total.shape[1] // PIECES
    copies = []
    for piece in range(PIECES):
        part = pl.ds(piece * wide, wide)
        value = product(weight, block[:, part])
        for ref in earlier:
            value = value + ref[:, part].astype(jnp.float32)
        total[:, part] = value
        copies.append(pltpu.make_async_copy(total.at[:, part], out.at[:, part], sems.at[piece]))
        copies[-1].start()
    for copy in copies:
        copy.wait()


def fixed_kernel(scalars, fixed, block, fixed_in, image_out, text_out, passed, total, sems):
    passed[...] = scalars[...]
    weight = weights(fixed[...], block[...], scalars)
    core_1 = on_core_1()

    @pl.when(core_1)
    def _():
        add_and_write(weight, block, [fixed_in], total, image_out, sems)

    @pl.when(jnp.logical_not(core_1))
    def _():
        add_and_write(weight, block, [fixed_in], total, text_out, sems)


def last_weights_kernel(scalars, moving, block, weight):
    weight[...] = weights(moving[...], block[...], scalars)


def last_kernel(weight, block, moving_in, other_in, image_in, text_in, image_out, text_out, total, sems):
    core_1 = on_core_1()

    @pl.when(core_1)
    def _():
        add_and_write(weight[...], block, [moving_in, other_in], total, text_out, sems)

    @pl.when(jnp.logical_not(core_1))
    def _():
        add_and_write(weight[...], block, [moving_in, other_in], total, image_out, sems)


def call(body, outs, n_in, products, **more):
    return pl.pallas_call(
        body,
        out_shape=outs,
        in_specs=more.pop("first", []) + [VMEM] * n_in + more.pop("more_in", []),
        out_specs=more.pop("out_specs", [VMEM] * len(outs)),
        compiler_params=pltpu.CompilerParams(vmem_limit_bytes=24 << 20),
        cost_estimate=pl.CostEstimate(flops=products * 85_000_000, bytes_accessed=1 << 20, transcendentals=0),
        **more,
    )


def local(image_emb, text_emb, log_scale, bias):
    n = lax.axis_size("dp") * lax.axis_size("mp")
    same = [(i, (i + 2) % n if i % 2 else (i - 2) % n) for i in range(n)]
    cross = [(i, (i - 1) % n if i % 2 == 0 else (i + 1) % n) for i in range(n)]
    split = [(i, (i + 3) % n if i % 2 == 0 else (i - 3) % n) for i in range(n)]
    swap = [(i, i ^ 1) for i in range(n)]
    shape = image_emb.shape
    block = pltpu.VMEM(shape, jnp.bfloat16)
    total = pltpu.VMEM(shape, jnp.float32)
    grad = jax.ShapeDtypeStruct(shape, jnp.float32)
    writes = dict(scratch_shapes=[pltpu.VMEM(shape, jnp.float32), pltpu.SemaphoreType.DMA((PIECES,))])

    moving, fixed = pl.pallas_call(
        choose_kernel,
        out_shape=[block, block],
        in_specs=[HBM, HBM],
        out_specs=[VMEM, VMEM],
        scratch_shapes=[pltpu.SemaphoreType.DMA((2,))],
    )(pltpu.with_memory_space_constraint(image_emb, pltpu.HBM), pltpu.with_memory_space_constraint(text_emb, pltpu.HBM))

    block2 = lax.ppermute(moving, AXES, same)
    row = pltpu.VMEM((2, shape[0]), jnp.float32)
    pair = pltpu.VMEM((2,) + shape, jnp.bfloat16)
    scalars, fixed_sum, moving_sum, fixed, both = call(own_kernel, [row, total, total, block, pair], 2, 4, first=[SMEM, SMEM])(
        log_scale, bias, fixed, moving
    )
    block3 = lax.ppermute(fixed, AXES, split)
    swapped = lax.ppermute(both, AXES, swap)
    block4 = lax.ppermute(block2, AXES, same)
    block5 = lax.ppermute(block3, AXES, cross)

    (fixed_sum,) = call(first_kernel, [total], 4, 150)(scalars, fixed, block2, fixed_sum)
    fixed_sum, other_sum = call(second_kernel, [total, total], 5, 4)(scalars, fixed, swapped, block2, fixed_sum)
    fixed_sum, other_sum = call(third_kernel, [total, total], 6, 4)(scalars, fixed, swapped, block3, fixed_sum, other_sum)
    (other_sum,) = call(other_kernel, [block], 4, 2)(scalars, swapped, block4, other_sum)
    other_sum = lax.ppermute(other_sum, AXES, swap)
    image_grad, text_grad, scalars = call(fixed_kernel, [grad, grad, row], 4, 2, out_specs=[HBM, HBM, VMEM], **writes)(
        scalars, fixed, block4, fixed_sum
    )
    (weight,) = call(last_weights_kernel, [pltpu.VMEM((shape[0], shape[0]), jnp.bfloat16)], 3, 1)(scalars, moving, block5)
    image_grad, text_grad = call(
        last_kernel, [grad, grad], 4, 1, more_in=[HBM, HBM], out_specs=[HBM, HBM], input_output_aliases={4: 0, 5: 1}, **writes
    )(weight, block5, moving_sum, other_sum, image_grad, text_grad)
    return (image_grad, text_grad)


def solution(mesh):
    return jax.shard_map(
        local,
        mesh=mesh,
        in_specs=(P(("dp", "mp"), None), P(("dp", "mp"), None), P(), P()),
        out_specs=(P(("dp", "mp"), None), P(("dp", "mp"), None)),
        check_vma=False,
    )
```

```python
import jax
import jax.numpy as jnp
from jax import lax
from jax.experimental import pallas as pl
from jax.experimental.pallas import tpu as pltpu
from jax.sharding import PartitionSpec as P

AXES = ("dp", "mp")
VMEM = pl.BlockSpec(memory_space=pltpu.VMEM)
HBM = pl.BlockSpec(memory_space=pltpu.HBM)
PIECES = 3
BAND = 128
WAIT = 150
NT = (((1,), (1,)), ((), ()))


def on_core_1():
    return lax.rem(lax.axis_index("mp"), 2) == 1


def place_in_band():
    count = lax.axis_size("dp") * lax.axis_size("mp")
    band = min(BAND, count)
    return lax.rem(lax.axis_index("dp") * lax.axis_size("mp") + lax.axis_index("mp"), band)


def weights(fixed, moving, scalars, own=False):
    inner = lax.dot_general(fixed, moving, NT, preferred_element_type=jnp.float32)
    scale, bias = scalars[0:1, :], scalars[1:2, :]
    chance = jax.nn.sigmoid(scale * inner + bias)
    if own:
        row_ids = lax.broadcasted_iota(jnp.int32, inner.shape, 0)
        col_ids = lax.broadcasted_iota(jnp.int32, inner.shape, 1)
        chance = chance - jnp.where(row_ids == col_ids, 1.0, 0.0)
    return (scale * chance).astype(jnp.bfloat16)


def product(left, right):
    return jnp.dot(left, right, preferred_element_type=jnp.float32)


def parts_of(array):
    wide = array.shape[1] // PIECES
    return [pl.ds(piece * wide, wide) for piece in range(PIECES)]


def choose_kernel(image, text, moving, fixed, sems):
    def copies(first, second):
        one = pltpu.make_async_copy(first, moving, sems.at[0])
        two = pltpu.make_async_copy(second, fixed, sems.at[1])
        one.start()
        two.start()
        one.wait()
        two.wait()

    core_1 = on_core_1()

    @pl.when(core_1)
    def _():
        copies(text, image)

    @pl.when(jnp.logical_not(core_1))
    def _():
        copies(image, text)


def own_kernel(log_scale, bias, fixed, moving, scalars, fixed_sum, moving_sum, both, fixed_copy):
    fixed_copy[...] = fixed[...]
    both[0] = fixed[...]
    both[1] = moving[...]
    scalars[0:1, :] = jnp.exp(jnp.broadcast_to(log_scale[...], (1, scalars.shape[1])))
    scalars[1:2, :] = jnp.broadcast_to(bias[...], (1, scalars.shape[1]))
    fixed_sum[...] = product(weights(fixed[...], moving[...], scalars, True), moving[...])
    moving_sum[...] = product(weights(moving[...], fixed[...], scalars, True), fixed[...])


def first_kernel(scalars, fixed, block, fixed_in, fixed_sum):
    fixed_sum[...] = fixed_in[...] + product(weights(fixed[...], block[...], scalars), block[...])


def first_hop_kernel(image, text, direct, block):
    core_1 = on_core_1()

    @pl.when(core_1)
    def _():
        block[...] = text[...]

    @pl.when(jnp.logical_not(core_1))
    def _():
        block[...] = image[...]


def middle_kernel(scalars, fixed, swapped, block2, block3, fixed_in, fixed_sum, other_sum):
    second, other = swapped.at[0], swapped.at[1]
    fixed_second = weights(fixed[...], second[...], scalars)
    other_2 = weights(other[...], block2[...], scalars)
    fixed_3 = weights(fixed[...], block3[...], scalars)
    other_3 = weights(other[...], block3[...], scalars)
    for part in parts_of(fixed_sum):
        fixed_sum[:, part] = fixed_in[:, part] + product(fixed_second, second[:, part]) + product(fixed_3, block3[:, part])
        other_sum[:, part] = product(other_2, block2[:, part]) + product(other_3, block3[:, part])


def other_kernel(scalars, fixed, swapped, forwarded, direct, other_in, other_sum, block, fixed_weight):
    block[...] = jnp.where(place_in_band() == 1, direct[...], forwarded[...])
    weight = weights(swapped[1], block[...], scalars)
    fixed_weight[...] = weights(fixed[...], block[...], scalars)
    for part in parts_of(other_sum):
        other_sum[:, part] = (other_in[:, part] + product(weight, block[:, part])).astype(other_sum.dtype)


def fixed_kernel(weight, block, fixed_in, passed_in, fixed_sum, passed):
    passed[...] = passed_in[...]
    for part in parts_of(fixed_sum):
        fixed_sum[:, part] = fixed_in[:, part] + product(weight[...], block[:, part])


def fifth_kernel(scalars, moving, forwarded, direct, weight, block):
    block[...] = jnp.where(place_in_band() == 0, direct[...], forwarded[...])
    weight[...] = weights(moving[...], block[...], scalars)


def last_kernel(weight, block, moving_in, other_in, fixed_sum, image_out, text_out, total, sems):
    def finish(fixed_out, moving_out):
        copies = [pltpu.make_async_copy(fixed_sum, fixed_out, sems.at[PIECES])]
        copies[0].start()
        for piece, part in enumerate(parts_of(total)):
            earlier = moving_in[:, part] + other_in[:, part].astype(jnp.float32)
            total[:, part] = earlier + product(weight[...], block[:, part])
            copies.append(pltpu.make_async_copy(total.at[:, part], moving_out.at[:, part], sems.at[piece]))
            copies[-1].start()
        for copy in copies:
            copy.wait()

    core_1 = on_core_1()

    @pl.when(core_1)
    def _():
        finish(image_out, text_out)

    @pl.when(jnp.logical_not(core_1))
    def _():
        finish(text_out, image_out)


def call(body, outs, n_in, products, **more):
    return pl.pallas_call(
        body,
        out_shape=outs,
        in_specs=[VMEM] * n_in + more.pop("more_in", []),
        out_specs=more.pop("out_specs", [VMEM] * len(outs)),
        compiler_params=pltpu.CompilerParams(vmem_limit_bytes=24 << 20),
        cost_estimate=pl.CostEstimate(flops=products * 85_000_000, bytes_accessed=1 << 20, transcendentals=0),
        **more,
    )


def local(image_emb, text_emb, log_scale, bias):
    n = lax.axis_size("dp") * lax.axis_size("mp")
    same = [(i, (i + 2) % n if i % 2 else (i - 2) % n) for i in range(n)]
    cross = [(i, (i - 1) % n if i % 2 == 0 else (i + 1) % n) for i in range(n)]
    split = [(i, (i + 3) % n if i % 2 == 0 else (i - 3) % n) for i in range(n)]
    swap = [(i, i ^ 1) for i in range(n)]
    band = min(BAND, n)
    starts = range(0, n, band)
    fourth = [((b - 3) % n, b + 1) for b in starts]
    fifth = [((b - 4) % n, b) for b in starts]
    same_but_direct = [(i, j) for i, j in same if j not in [b + 1 for b in starts]]
    cross_but_direct = [(i, j) for i, j in cross if j not in starts]
    shape = image_emb.shape
    block = pltpu.VMEM(shape, jnp.bfloat16)
    total = pltpu.VMEM(shape, jnp.float32)
    grad = jax.ShapeDtypeStruct(shape, jnp.float32)
    moving, fixed = pl.pallas_call(
        choose_kernel,
        out_shape=[block, block],
        in_specs=[HBM, HBM],
        out_specs=[VMEM, VMEM],
        scratch_shapes=[pltpu.SemaphoreType.DMA((2,))],
    )(pltpu.with_memory_space_constraint(image_emb, pltpu.HBM), pltpu.with_memory_space_constraint(text_emb, pltpu.HBM))

    image2 = lax.ppermute(image_emb, AXES, [(i, j) for i, j in same if i % 2 == 0])
    text2 = lax.ppermute(text_emb, AXES, [(i, j) for i, j in same if i % 2 == 1])
    row = pltpu.VMEM((2, shape[0]), jnp.float32)
    square = pltpu.VMEM((shape[0], shape[0]), jnp.bfloat16)
    pair = pltpu.VMEM((2,) + shape, jnp.bfloat16)
    scalars, fixed_sum, moving_sum, both, fixed_copy = call(own_kernel, [row, total, total, pair, block], 4, 4)(
        log_scale.reshape(1, 1), bias.reshape(1, 1), fixed, moving
    )
    block3 = lax.ppermute(fixed_copy, AXES, split)
    swapped = lax.ppermute(both, AXES, swap)
    direct4 = lax.ppermute(text_emb, AXES, fourth)
    direct5 = lax.ppermute(fixed_copy, AXES, fifth)
    (block2,) = call(first_hop_kernel, [block], 3, WAIT)(image2, text2, direct4)
    block4 = lax.ppermute(block2, AXES, same_but_direct)
    block5 = lax.ppermute(block3, AXES, cross_but_direct)

    (fixed_sum,) = call(first_kernel, [total], 4, WAIT)(scalars, fixed, block2, fixed_sum)
    fixed_sum, other_sum = call(middle_kernel, [total, total], 6, 8)(scalars, fixed, swapped, block2, block3, fixed_sum)
    other_sum, block4, weight4 = call(other_kernel, [block, block, square], 6, 3)(
        scalars, fixed, swapped, block4, direct4, other_sum
    )
    other_sum = lax.ppermute(other_sum, AXES, swap)
    fixed_sum, scalars = call(fixed_kernel, [total, row], 4, 1)(weight4, block4, fixed_sum, scalars)
    weight5, block5 = call(fifth_kernel, [square, block], 4, 1)(scalars, moving, block5, direct5)
    image_grad, text_grad = call(
        last_kernel,
        [grad, grad],
        5,
        1,
        out_specs=[HBM, HBM],
        scratch_shapes=[pltpu.VMEM(shape, jnp.float32), pltpu.SemaphoreType.DMA((PIECES + 1,))],
    )(weight5, block5, moving_sum, other_sum, fixed_sum)
    return (image_grad, text_grad)


def solution(mesh):
    return jax.shard_map(
        local,
        mesh=mesh,
        in_specs=(P(("dp", "mp"), None), P(("dp", "mp"), None), P(), P()),
        out_specs=(P(("dp", "mp"), None), P(("dp", "mp"), None)),
        check_vma=False,
    )
```

```python
import jax
import jax.numpy as jnp
from jax import lax
from jax.experimental import pallas as pl
from jax.experimental.pallas import tpu as pltpu
from jax.sharding import PartitionSpec as P

AXES = ("dp", "mp")
VMEM = pl.BlockSpec(memory_space=pltpu.VMEM)
HBM = pl.BlockSpec(memory_space=pltpu.HBM)
PIECES = 3
BAND = 128
WAIT = 150
WAIT2 = 20
NT = (((1,), (1,)), ((), ()))


def on_core_1():
    return lax.rem(lax.axis_index("mp"), 2) == 1


def place_in_band():
    count = lax.axis_size("dp") * lax.axis_size("mp")
    band = min(BAND, count)
    return lax.rem(lax.axis_index("dp") * lax.axis_size("mp") + lax.axis_index("mp"), band)


def weights(fixed, moving, scalars, own=False):
    inner = lax.dot_general(fixed, moving, NT, preferred_element_type=jnp.float32)
    scale, bias = scalars[0:1, :], scalars[1:2, :]
    chance = jax.nn.sigmoid(scale * inner + bias)
    if own:
        row_ids = lax.broadcasted_iota(jnp.int32, inner.shape, 0)
        col_ids = lax.broadcasted_iota(jnp.int32, inner.shape, 1)
        chance = chance - jnp.where(row_ids == col_ids, 1.0, 0.0)
    return (scale * chance).astype(jnp.bfloat16)


def product(left, right):
    return jnp.dot(left, right, preferred_element_type=jnp.float32)


def parts_of(array):
    wide = array.shape[1] // PIECES
    return [pl.ds(piece * wide, wide) for piece in range(PIECES)]


def choose_kernel(image, text, moving, fixed, sems):
    def copies(first, second):
        one = pltpu.make_async_copy(first, moving, sems.at[0])
        two = pltpu.make_async_copy(second, fixed, sems.at[1])
        one.start()
        two.start()
        one.wait()
        two.wait()

    core_1 = on_core_1()

    @pl.when(core_1)
    def _():
        copies(text, image)

    @pl.when(jnp.logical_not(core_1))
    def _():
        copies(image, text)


def own_kernel(log_scale, bias, fixed, moving, scalars, fixed_sum, moving_sum, both, fixed_copy):
    fixed_copy[...] = fixed[...]
    both[0] = fixed[...]
    both[1] = moving[...]
    scalars[0:1, :] = jnp.exp(jnp.broadcast_to(log_scale[...], (1, scalars.shape[1])))
    scalars[1:2, :] = jnp.broadcast_to(bias[...], (1, scalars.shape[1]))
    fixed_sum[...] = product(weights(fixed[...], moving[...], scalars, True), moving[...])
    moving_sum[...] = product(weights(moving[...], fixed[...], scalars, True), fixed[...])


def first_kernel(scalars, fixed, block, fixed_in, fixed_sum):
    fixed_sum[...] = fixed_in[...] + product(weights(fixed[...], block[...], scalars), block[...])


def first_hop_kernel(image, text, block):
    core_1 = on_core_1()

    @pl.when(core_1)
    def _():
        block[...] = text[...]

    @pl.when(jnp.logical_not(core_1))
    def _():
        block[...] = image[...]


def wait_kernel(direct, row):
    row[...] = direct[0 : row.shape[0], 0 : row.shape[1]]


def second_hop_kernel(block, row, block_copy):
    block_copy[...] = block[...]


def middle_kernel(scalars, fixed, swapped, block2, block3, fixed_in, fixed_sum, other_sum):
    second, other = swapped.at[0], swapped.at[1]
    fixed_second = weights(fixed[...], second[...], scalars)
    other_2 = weights(other[...], block2[...], scalars)
    fixed_3 = weights(fixed[...], block3[...], scalars)
    other_3 = weights(other[...], block3[...], scalars)
    for part in parts_of(fixed_sum):
        fixed_sum[:, part] = fixed_in[:, part] + product(fixed_second, second[:, part]) + product(fixed_3, block3[:, part])
        other_sum[:, part] = product(other_2, block2[:, part]) + product(other_3, block3[:, part])


def other_kernel(scalars, fixed, swapped, forwarded, direct, other_in, other_sum, block, fixed_weight):
    block[...] = jnp.where(place_in_band() == 1, direct[...], forwarded[...])
    weight = weights(swapped[1], block[...], scalars)
    fixed_weight[...] = weights(fixed[...], block[...], scalars)
    for part in parts_of(other_sum):
        other_sum[:, part] = (other_in[:, part] + product(weight, block[:, part])).astype(other_sum.dtype)


def fixed_kernel(weight, block, fixed_in, passed_in, fixed_sum, passed):
    passed[...] = passed_in[...]
    for part in parts_of(fixed_sum):
        fixed_sum[:, part] = fixed_in[:, part] + product(weight[...], block[:, part])


def fifth_kernel(scalars, moving, forwarded, direct, weight, block):
    block[...] = jnp.where(place_in_band() == 0, direct[...], forwarded[...])
    weight[...] = weights(moving[...], block[...], scalars)


def last_kernel(weight, block, moving_in, other_in, fixed_sum, image_out, text_out, total, sems):
    def finish(fixed_out, moving_out):
        copies = [pltpu.make_async_copy(fixed_sum, fixed_out, sems.at[PIECES])]
        copies[0].start()
        for piece, part in enumerate(parts_of(total)):
            earlier = moving_in[:, part] + other_in[:, part].astype(jnp.float32)
            total[:, part] = earlier + product(weight[...], block[:, part])
            copies.append(pltpu.make_async_copy(total.at[:, part], moving_out.at[:, part], sems.at[piece]))
            copies[-1].start()
        for copy in copies:
            copy.wait()

    core_1 = on_core_1()

    @pl.when(core_1)
    def _():
        finish(image_out, text_out)

    @pl.when(jnp.logical_not(core_1))
    def _():
        finish(text_out, image_out)


def call(body, outs, n_in, products, **more):
    return pl.pallas_call(
        body,
        out_shape=outs,
        in_specs=[VMEM] * n_in + more.pop("more_in", []),
        out_specs=more.pop("out_specs", [VMEM] * len(outs)),
        compiler_params=pltpu.CompilerParams(vmem_limit_bytes=24 << 20),
        cost_estimate=pl.CostEstimate(flops=products * 85_000_000, bytes_accessed=1 << 20, transcendentals=0),
        **more,
    )


def local(image_emb, text_emb, log_scale, bias):
    n = lax.axis_size("dp") * lax.axis_size("mp")
    same = [(i, (i + 2) % n if i % 2 else (i - 2) % n) for i in range(n)]
    cross = [(i, (i - 1) % n if i % 2 == 0 else (i + 1) % n) for i in range(n)]
    split = [(i, (i + 3) % n if i % 2 == 0 else (i - 3) % n) for i in range(n)]
    swap = [(i, i ^ 1) for i in range(n)]
    band = min(BAND, n)
    starts = range(0, n, band)
    fourth = [((b - 3) % n, b + 1) for b in starts]
    fifth = [((b - 4) % n, b) for b in starts]
    same_but_direct = [(i, j) for i, j in same if j not in [b + 1 for b in starts]]
    cross_but_direct = [(i, j) for i, j in cross if j not in starts]
    shape = image_emb.shape
    block = pltpu.VMEM(shape, jnp.bfloat16)
    total = pltpu.VMEM(shape, jnp.float32)
    grad = jax.ShapeDtypeStruct(shape, jnp.float32)
    moving, fixed = pl.pallas_call(
        choose_kernel,
        out_shape=[block, block],
        in_specs=[HBM, HBM],
        out_specs=[VMEM, VMEM],
        scratch_shapes=[pltpu.SemaphoreType.DMA((2,))],
    )(pltpu.with_memory_space_constraint(image_emb, pltpu.HBM), pltpu.with_memory_space_constraint(text_emb, pltpu.HBM))

    image2 = lax.ppermute(image_emb, AXES, [(i, j) for i, j in same if i % 2 == 0])
    text2 = lax.ppermute(text_emb, AXES, [(i, j) for i, j in same if i % 2 == 1])
    row = pltpu.VMEM((2, shape[0]), jnp.float32)
    square = pltpu.VMEM((shape[0], shape[0]), jnp.bfloat16)
    pair = pltpu.VMEM((2,) + shape, jnp.bfloat16)
    scalars, fixed_sum, moving_sum, both, fixed_copy = call(own_kernel, [row, total, total, pair, block], 4, 4)(
        log_scale.reshape(1, 1), bias.reshape(1, 1), fixed, moving
    )
    block3 = lax.ppermute(fixed_copy, AXES, split)
    swapped = lax.ppermute(both, AXES, swap)
    direct4 = lax.ppermute(text_emb, AXES, fourth)
    direct5 = lax.ppermute(fixed_copy, AXES, fifth)
    (block2,) = call(first_hop_kernel, [block], 2, 0)(image2, text2)
    block4 = lax.ppermute(block2, AXES, same_but_direct)
    (waited,) = call(wait_kernel, [pltpu.VMEM((16, 128), jnp.bfloat16)], 1, WAIT2)(direct4)
    (block3,) = call(second_hop_kernel, [block], 2, 0)(block3, waited)
    block5 = lax.ppermute(block3, AXES, cross_but_direct)

    (fixed_sum,) = call(first_kernel, [total], 4, 70)(scalars, fixed, block2, fixed_sum)
    fixed_sum, other_sum = call(middle_kernel, [total, total], 6, 8)(scalars, fixed, swapped, block2, block3, fixed_sum)
    other_sum, block4, weight4 = call(other_kernel, [block, block, square], 6, 3)(
        scalars, fixed, swapped, block4, direct4, other_sum
    )
    other_sum = lax.ppermute(other_sum, AXES, swap)
    fixed_sum, scalars = call(fixed_kernel, [total, row], 4, 1)(weight4, block4, fixed_sum, scalars)
    weight5, block5 = call(fifth_kernel, [square, block], 4, 1)(scalars, moving, block5, direct5)
    image_grad, text_grad = call(
        last_kernel,
        [grad, grad],
        5,
        1,
        out_specs=[HBM, HBM],
        scratch_shapes=[pltpu.VMEM(shape, jnp.float32), pltpu.SemaphoreType.DMA((PIECES + 1,))],
    )(weight5, block5, moving_sum, other_sum, fixed_sum)
    return (image_grad, text_grad)


def solution(mesh):
    return jax.shard_map(
        local,
        mesh=mesh,
        in_specs=(P(("dp", "mp"), None), P(("dp", "mp"), None), P(), P()),
        out_specs=(P(("dp", "mp"), None), P(("dp", "mp"), None)),
        check_vma=False,
    )
```
